32 devices in a mesh: row: 8 (over z, y), col: 4 (over x, core).
Axes of the slice: x: 2, y: 2, z: 4, core: 2. Of those that a mesh axis runs over, the one named last changes fastest.
Arguments:
- features: bfloat16 [8192, 256], P('row', 'col'), may hold values from -600 to 600
- tile_vals: bfloat16 [1280, 128, 128], P('row'), may hold values from -0.125 to 0.125
- tile_rows: int32 [8, 160], P('row'), may hold values from 0 to 7
- tile_srcs: int32 [8, 160], P('row'), may hold values from 0 to 23, as said below
- tile_count: int32 [8], P('row'), may hold values from 20 to 160, as said below
- needed: int32 [8, 8, 2], P('row'), may hold values from 0 to 7, as said below
- hop_noise: float32 [2, 8192, 256], P(None, 'row', 'col'), may hold values from -0.24 to 0.24
- enc_weight: bfloat16 [3, 256, 256], replicated, may hold values from -3.59375 to 3.59375
Outputs:
- encoded: bfloat16 [8192, 256], P('row', 'col')
The draws below stay inside these ranges and needn't reach their ends.
Inputs may be any that keep to these rules, and one draw needn't show every extreme that they name: `tile_count`: some row index has exactly 160 live slots; slots at or beyond a row index's count are ignored. `tile_srcs`: A value s below 8 names the row index's own block s; otherwise s = 8 + o * 2 + c names entry c of needed for owner o, and o is never the row index itself. needed[d, o, :] are 2 distinct block indices among owner o's 8 blocks.
All inputs are finite; a program needn't handle non-finite values.
Results may differ from the reference program's by a relative error of at most 0.0053.
Values may be sent and summed in bfloat16 or wider, within the bound.
A program may use at most 64 MiB of HBM per device.

```python
import jax
import jax.numpy as jnp
from jax import lax

F = 256
BLK = 128
BPD = 8
TPD = 160
CAP = 2
HOPS = 2
NODES = 8192
TILES = 1280
N_ROW = 8


def draw_features(key, part):
    first, second, third = jax.random.split(key, 3)
    columns = jnp.arange(F, dtype=jnp.float32)
    column_scale = 10.0 ** (columns / (F - 1)) * jnp.exp(jax.random.uniform(second, (F,), minval=-0.35, maxval=0.35))
    base = jnp.clip(jax.random.normal(first, (NODES, F)), -4.0, 4.0)
    row_scale = 10.0 ** jax.random.uniform(third, (NODES, 1))
    return (base * column_scale[None, :] * row_scale).astype(jnp.bfloat16)


def draw_tile_count(key, part):
    first, second = jax.random.split(jax.random.fold_in(key, 11))
    shifts = jax.random.randint(first, (N_ROW,), 0, 4)
    counts = TPD // 2 ** shifts
    busiest = jax.random.randint(second, (), 0, N_ROW)
    return jnp.where(jnp.arange(N_ROW) == busiest, TPD, counts).astype(jnp.int32)


def draw_tile_rows(key, part):
    return jax.random.randint(jax.random.fold_in(key, 12), (N_ROW, TPD), 0, BPD).astype(jnp.int32)


def draw_tile_srcs(key, part):
    first, second, third, fourth = jax.random.split(jax.random.fold_in(key, 13), 4)
    local = jax.random.randint(first, (N_ROW, TPD), 0, 3) == 0
    own_block = jax.random.randint(second, (N_ROW, TPD), 0, BPD)
    offset = jax.random.randint(third, (N_ROW, TPD), 1, N_ROW)
    owner = (jnp.arange(N_ROW)[:, None] + offset) % N_ROW
    slot = jax.random.randint(fourth, (N_ROW, TPD), 0, CAP)
    return jnp.where(local, own_block, BPD + owner * CAP + slot).astype(jnp.int32)


def draw_needed(key, part):
    scores = jax.random.randint(jax.random.fold_in(key, 14), (N_ROW, N_ROW, BPD), 0, 2 ** 20)
    scores = scores * BPD + jnp.arange(BPD)[None, None, :]
    order = jnp.argsort(scores, axis=-1, stable=True)
    return order[:, :, :CAP].astype(jnp.int32)


def steps_of(stream_key, shape, pieces, low, largest):
    def one(dim, blocks):
        draws = jax.random.uniform(jax.random.fold_in(jax.random.fold_in(stream_key, 6), dim), (blocks,), jnp.float32, low / len(pieces), largest / len(pieces))
        return jnp.repeat(jnp.exp(draws), shape[dim] // blocks).reshape((-1,) + (1,) * (len(shape) - dim - 1))

    level = one(*pieces[0])
    for cut in pieces[1:]:
        level = level * one(*cut)
    return level


def noise(rng, dims, deviation, most, cuts=(), kind=jnp.bfloat16):
    drawn = deviation * jax.random.normal(rng, dims, jnp.float32)
    if cuts:
        drawn = drawn * steps_of(rng, dims, cuts, -0.22, 0.18)
    return jnp.clip(drawn, -most, most).astype(kind)


def setup_inputs(seed: int = 0) -> dict:
    arg_keys = jax.random.split(jax.random.key(seed), 9)
    features = draw_features(jax.random.fold_in(arg_keys[8], 71), 0)
    tile_vals = noise(arg_keys[1], (TILES, BLK, BLK), (BLK * TPD // BPD) ** -0.5, 0.125, ((0, 8),))
    tile_rows = draw_tile_rows(jax.random.fold_in(arg_keys[8], 71), 0)
    tile_srcs = draw_tile_srcs(jax.random.fold_in(arg_keys[8], 71), 0)
    tile_count = draw_tile_count(jax.random.fold_in(arg_keys[8], 71), 0)
    needed = draw_needed(jax.random.fold_in(arg_keys[8], 71), 0)
    hop_noise = noise(arg_keys[6], (HOPS, NODES, F), 0.04, 0.24, ((1, 8), (2, 4)), jnp.float32)
    enc_weight = noise(arg_keys[7], (HOPS + 1, F, F), 0.6, 3.59375)
    return dict(features=features, tile_vals=tile_vals, tile_rows=tile_rows, tile_srcs=tile_srcs, tile_count=tile_count, needed=needed, hop_noise=hop_noise, enc_weight=enc_weight)


epsilon = 1e-06

def normalize(values):
    squares = lax.optimization_barrier(jnp.sum(values * values, axis=1, keepdims=True))
    return (values / jnp.sqrt(squares + epsilon)).astype(jnp.bfloat16)

def aggregate(previous, tile_vals, tile_rows, tile_srcs, tile_count, needed):
    blocks = previous.astype(jnp.float32).reshape(N_ROW * BPD, BLK, F)
    values = tile_vals.reshape(N_ROW, TPD, BLK, BLK)

    def one_device(device):
        sources = tile_srcs[device]
        remote = jnp.maximum(sources - BPD, 0)
        owner = (remote // CAP).astype(jnp.int32)
        slot = (remote % CAP).astype(jnp.int32)
        far_block = owner * BPD + needed[device][owner, slot]
        near_block = device * BPD + sources
        index = jnp.where(sources < BPD, near_block, far_block).astype(jnp.int32)
        picked = blocks[index]
        products = jnp.einsum('tij,tjf->tif', values[device].astype(jnp.float32), picked, precision=lax.Precision.HIGHEST)
        live = jnp.arange(TPD, dtype=jnp.int32) < tile_count[device]
        onehot = ((tile_rows[device][:, None] == jnp.arange(BPD, dtype=jnp.int32)[None, :]) & live[:, None]).astype(jnp.float32)
        return jnp.einsum('tr,tif->rif', onehot, products, precision=lax.Precision.HIGHEST)
    summed = lax.map(one_device, jnp.arange(N_ROW, dtype=jnp.int32))
    return summed.reshape(N_ROW * BPD * BLK, F)

def reference(features, tile_vals, tile_rows, tile_srcs, tile_count, needed, hop_noise, enc_weight):
    current = normalize(features.astype(jnp.float32))
    layers = [current]
    for hop_index in range(HOPS):
        gathered = aggregate(current, tile_vals, tile_rows, tile_srcs, tile_count, needed)
        current = normalize(gathered + hop_noise[hop_index])
        layers.append(current)
    stacked = jnp.stack(layers).astype(jnp.float32)
    encoded = jnp.einsum('kri,kio->ro', stacked, enc_weight.astype(jnp.float32), precision=lax.Precision.HIGHEST)
    return encoded.astype(jnp.bfloat16)
```

```python
import functools

import jax
import jax.numpy as jnp
from jax import lax
from jax.experimental import pallas as pl
from jax.experimental.pallas import tpu as pltpu
from jax.sharding import PartitionSpec as P

BLK = 128
BPD = 8
CAP = 2
HOPS = 2
PAIRS = BPD // 2
MESH = pl.DeviceIdType.MESH
EPSILON = 1e-06


def kernel(n, nc, prev, head, wanted, feat, tiles, noise, weight, out,
           vals, sums, dense, noise_v, weight_v, squares, xs, hd, send, recv, wanted_v, wanted_s,
           heads, head_w, acc, enc,
           local_sem, wanted_send, wanted_recv, sq_send, sq_recv, row_send, row_recv, col_send, col_recv, table_sem):
    me = lax.axis_index("row")
    col = lax.axis_index("col")
    width = feat.shape[1]
    slots = vals.shape[0]
    f32, bf16 = jnp.float32, jnp.bfloat16

    vals_copy = pltpu.make_async_copy(tiles, vals, local_sem.at[0])
    noise_copy = pltpu.make_async_copy(noise, noise_v, local_sem.at[1])
    weight_copy = pltpu.make_async_copy(weight, weight_v, local_sem.at[2])
    vals_copy.start()
    noise_copy.start()
    weight_copy.start()

    barrier = pltpu.get_barrier_semaphore()

    def greet_row(k, c):
        pl.semaphore_signal(barrier, inc=1, device_id={"row": lax.rem(me + k, n)}, device_id_type=MESH)
        return c

    lax.fori_loop(1, n, greet_row, 0)
    for k in range(1, nc):
        pl.semaphore_signal(barrier, inc=1, device_id={"col": lax.rem(col + k, nc)}, device_id_type=MESH)

    left = lax.broadcasted_iota(jnp.int32, (BLK, 2 * width), 1) < width
    zero_tile = jnp.zeros((BLK, 2 * width), f32)

    def stat(stage, x):
        for j in range(PAIRS):
            t = (x[j] * x[j]).T
            squares[stage, 0, 2 * j : 2 * j + 1, :] = jnp.sum(t[:width], axis=0, keepdims=True)
            squares[stage, 0, 2 * j + 1 : 2 * j + 2, :] = jnp.sum(t[width:], axis=0, keepdims=True)
            xs[j] = x[j]

    def square_copy(stage, k):
        return pltpu.make_async_remote_copy(
            src_ref=squares.at[stage, 0], dst_ref=squares.at[stage, k],
            send_sem=sq_send.at[stage, k], recv_sem=sq_recv.at[stage, k],
            device_id={"col": lax.rem(col + k, nc)}, device_id_type=MESH)

    def head_copy(stage, k):
        return pltpu.make_async_remote_copy(
            src_ref=heads.at[stage, 0], dst_ref=heads.at[stage, k],
            send_sem=col_send.at[stage, k], recv_sem=col_recv.at[stage, k],
            device_id={"col": lax.rem(col + k, nc)}, device_id_type=MESH)

    def wanted_copy(k):
        peer = lax.rem(me + k, n)
        return pltpu.make_async_remote_copy(
            src_ref=wanted.at[peer], dst_ref=wanted_v.at[k],
            send_sem=wanted_send.at[k], recv_sem=wanted_recv.at[k],
            device_id={"row": peer}, device_id_type=MESH)

    def row_copy(hop, k):
        return pltpu.make_async_remote_copy(
            src_ref=send.at[k], dst_ref=recv.at[hop, k],
            send_sem=row_send.at[hop, k], recv_sem=row_recv.at[hop, k],
            device_id={"row": lax.rem(me + k, n)}, device_id_type=MESH)

    def row_loop(body):
        def step(k, c):
            body(k)
            return c
        lax.fori_loop(1, n, step, 0)

    def normalized(stage):
        for k in range(1, nc):
            square_copy(stage, k).wait_recv()
        total = squares[stage, 0]
        for k in range(1, nc):
            total = total + squares[stage, k]
        inverse = 1.0 / jnp.sqrt(total + EPSILON)
        for j in range(PAIRS):
            both = jnp.concatenate(
                [jnp.broadcast_to(inverse[2 * j : 2 * j + 1], (width, BLK)),
                 jnp.broadcast_to(inverse[2 * j + 1 : 2 * j + 2], (width, BLK))], axis=0).T
            h = (xs[j] * both).astype(bf16)
            heads[stage, 0, j] = h
            if stage < HOPS:
                h = h.astype(f32)
                turned = pltpu.roll(h, width, 1)
                hd[2 * j] = jnp.where(left, h, turned).astype(bf16)
                hd[2 * j + 1] = jnp.where(left, turned, h).astype(bf16)

    def send_rows(hop):
        def body(k):
            first = wanted_s[n - k, 0, 0]
            second = wanted_s[n - k, 0, 1]
            a = hd[first].astype(f32)
            b = hd[second].astype(f32)
            if hop > 0:
                row_copy(hop - 1, k).wait_send()
            send[k] = jnp.where(left, a, b).astype(bf16)
            row_copy(hop, k).start()
        row_loop(body)

    def spread(packed):
        p = packed.astype(f32)
        return jnp.concatenate([jnp.where(left, p, 0.0), jnp.where(left, 0.0, p)], axis=0).astype(bf16)

    def add_encoded(stage, k):
        source = lax.rem(col + nc - k, nc)
        e = head_w[stage, pl.ds(pl.multiple_of(source * width, width), width), :].astype(f32)
        mask = left[:width]
        w = jnp.concatenate([jnp.where(mask, e, 0.0), jnp.where(mask, 0.0, e)], axis=0).astype(bf16)
        enc[...] += jnp.dot(heads[stage, k].reshape(PAIRS * BLK, 2 * width), w, preferred_element_type=f32)

    diag = lax.broadcasted_iota(jnp.int32, (width, 2 * width), 0)
    lane = lax.broadcasted_iota(jnp.int32, (width, 2 * width), 1)
    twice = ((lane == diag) | (lane == diag + width)).astype(f32).astype(bf16)
    x = []
    for j in range(PAIRS):
        both = jnp.dot(feat[2 * j * BLK : (2 * j + 2) * BLK, :], twice, preferred_element_type=f32)
        x.append(jnp.where(left, both[:BLK], both[BLK:]))
    stat(0, x)

    pl.semaphore_wait(barrier, n - 1 + nc - 1)
    for k in range(1, nc):
        square_copy(0, k).start()
    row_loop(lambda k: wanted_copy(k).start())
    sums[slots] = zero_tile
    row_loop(lambda k: wanted_copy(k).wait_recv())
    table = pltpu.make_async_copy(wanted_v.at[pl.ds(1, n - 1)], wanted_s.at[pl.ds(1, n - 1)], table_sem.at[0])
    table.start()
    normalized(0)
    table.wait()
    send_rows(0)
    for k in range(1, nc):
        head_copy(0, k).start()

    vals_copy.wait()

    def link(t, c):
        sums[t] = vals[t].astype(f32) + sums[prev[t]]
        return c

    lax.fori_loop(0, slots, link, 0, unroll=4)

    def lay(q, c):
        for r in range(BPD):
            for h in range(2):
                dense[q, r * BLK : (r + 1) * BLK, h * BLK : (h + 1) * BLK] = (
                    sums[head[(2 * q + h) * BPD + r]].astype(bf16))
        return c

    lax.fori_loop(0, dense.shape[0], lay, 0)

    weight_copy.wait()
    depth = weight_v.shape[1]
    pick_row = lax.broadcasted_iota(jnp.int32, (depth, 2 * width), 0) - col * width
    pick_lane = lax.broadcasted_iota(jnp.int32, (depth, 2 * width), 1)
    pick = ((pick_lane == pick_row) | (pick_lane == pick_row + width)).astype(f32)
    pick = jnp.where((pick_row >= 0) & (pick_row < width), pick, 0.0).astype(bf16)
    for stage in range(HOPS + 1):
        head_w[stage] = jnp.dot(weight_v[stage], pick, preferred_element_type=f32).astype(bf16)
    enc[...] = jnp.zeros_like(enc)
    noise_copy.wait()

    for hop in range(HOPS):
        acc[...] = jnp.dot(dense[0], spread(heads[hop, 0, 0]), preferred_element_type=f32)
        for j in range(1, PAIRS):
            acc[...] += jnp.dot(dense[j], spread(heads[hop, 0, j]), preferred_element_type=f32)
        add_encoded(hop, 0)
        if hop > 0:
            for k in range(1, nc):
                head_copy(hop - 1, k).wait_recv()
                add_encoded(hop - 1, k)

        def arrive(k):
            row_copy(hop, k).wait_recv()
            owner = lax.rem(me + n - k, n)
            acc[...] += jnp.dot(dense[PAIRS + owner], spread(recv[hop, k]), preferred_element_type=f32)

        row_loop(arrive)
        x = []
        for j in range(PAIRS):
            a = acc[2 * j * BLK : (2 * j + 1) * BLK, :]
            b = acc[(2 * j + 1) * BLK : (2 * j + 2) * BLK, :]
            g = jnp.where(left, a, b) + pltpu.roll(jnp.where(left, b, a), width, 1)
            z = jnp.concatenate(
                [noise_v[hop, 2 * j * BLK : (2 * j + 1) * BLK, :],
                 noise_v[hop, (2 * j + 1) * BLK : (2 * j + 2) * BLK, :]], axis=1)
            x.append(g + z)
        stat(hop + 1, x)
        for k in range(1, nc):
            square_copy(hop + 1, k).start()
        normalized(hop + 1)
        if hop + 1 < HOPS:
            send_rows(hop + 1)
        for k in range(1, nc):
            head_copy(hop + 1, k).start()

    add_encoded(HOPS, 0)
    for stage in (HOPS - 1, HOPS):
        for k in range(1, nc):
            head_copy(stage, k).wait_recv()
            add_encoded(stage, k)
    for j in range(PAIRS):
        e = enc[j * BLK : (j + 1) * BLK, :]
        out[2 * j * BLK : (2 * j + 1) * BLK, :] = e[:, :width].astype(bf16)
        out[(2 * j + 1) * BLK : (2 * j + 2) * BLK, :] = pltpu.roll(e, width, 1)[:, :width].astype(bf16)

    row_loop(lambda k: wanted_copy(k).wait_send())
    row_loop(lambda k: row_copy(HOPS - 1, k).wait_send())
    for stage in range(HOPS + 1):
        for k in range(1, nc):
            square_copy(stage, k).wait_send()
            head_copy(stage, k).wait_send()


def shards(n, nc, features, tile_vals, tile_rows, tile_srcs, tile_count, needed, hop_noise, enc_weight):
    local_rows, width = features.shape
    slots = tile_vals.shape[0]
    cells = (BPD + n * CAP) * BPD
    order = jnp.arange(slots, dtype=jnp.int32)
    cell = tile_srcs[0] * BPD + tile_rows[0]
    same = (cell[:, None] == cell[None, :]) & (order[None, :] < order[:, None])
    prev = jnp.max(jnp.where(same, order[None, :], -1), axis=1)
    prev = jnp.where(prev < 0, slots, prev)
    mine = (cell[None, :] == jnp.arange(cells, dtype=jnp.int32)[:, None]) & (order < tile_count[0])[None, :]
    head = jnp.max(jnp.where(mine, order[None, :], -1), axis=1)
    head = jnp.where(head < 0, slots, head)
    wanted = jnp.pad(needed[0][:, None, :], ((0, 0), (0, 0), (0, BLK - CAP)))
    f32, bf16 = jnp.float32, jnp.bfloat16
    vmem = pl.BlockSpec(memory_space=pltpu.VMEM)
    smem = pl.BlockSpec(memory_space=pltpu.SMEM)
    anyspace = pl.BlockSpec(memory_space=pl.ANY)
    sem = pltpu.SemaphoreType.DMA
    pair = (BLK, 2 * width)
    return pl.pallas_call(
        functools.partial(kernel, n, nc),
        out_shape=jax.ShapeDtypeStruct((local_rows, width), bf16),
        in_specs=[smem, smem, anyspace, vmem, anyspace, anyspace, anyspace],
        out_specs=vmem,
        scratch_shapes=[
            pltpu.VMEM(tile_vals.shape, bf16),
            pltpu.VMEM((slots + 1, BLK, BLK), f32),
            pltpu.VMEM((PAIRS + n, local_rows, 2 * BLK), bf16),
            pltpu.VMEM(hop_noise.shape, f32),
            pltpu.VMEM(enc_weight.shape, bf16),
            pltpu.VMEM((HOPS + 1, nc, BPD, BLK), f32),
            pltpu.VMEM((PAIRS,) + pair, f32),
            pltpu.VMEM((BPD,) + pair, bf16),
            pltpu.VMEM((n,) + pair, bf16),
            pltpu.VMEM((HOPS, n) + pair, bf16),
            pltpu.VMEM((n, 1, BLK), jnp.int32),
            pltpu.SMEM((n, 1, BLK), jnp.int32),
            pltpu.VMEM((HOPS + 1, nc, PAIRS) + pair, bf16),
            pltpu.VMEM((HOPS + 1, enc_weight.shape[1], 2 * width), bf16),
            pltpu.VMEM((local_rows, 2 * width), f32),
            pltpu.VMEM((PAIRS * BLK, 2 * width), f32),
            sem((3,)),
            sem((n,)), sem((n,)),
            sem((HOPS + 1, nc)), sem((HOPS + 1, nc)),
            sem((HOPS, n)), sem((HOPS, n)),
            sem((HOPS + 1, nc)), sem((HOPS + 1, nc)),
            sem((1,)),
        ],
        compiler_params=pltpu.CompilerParams(
            collective_id=0, has_side_effects=True, vmem_limit_bytes=62 * 2**20),
    )(prev, head, wanted, features, tile_vals, hop_noise, enc_weight)


def solution(mesh):
    n, nc = mesh.shape["row"], mesh.shape["col"]
    in_specs = (
        P("row", "col"),
        P("row", None, None),
        P("row", None),
        P("row", None),
        P("row"),
        P("row", None, None),
        P(None, "row", "col"),
        P(),
    )
    return jax.shard_map(functools.partial(shards, n, nc), mesh=mesh, in_specs=in_specs,
                         out_specs=P("row", "col"), check_vma=False)
```

```python
import functools

import jax
import jax.numpy as jnp
from jax import lax
from jax.experimental import pallas as pl
from jax.experimental.pallas import tpu as pltpu
from jax.sharding import PartitionSpec as P

BLK = 128
BPD = 8
CAP = 2
HOPS = 2
PAIRS = BPD // 2
MESH = pl.DeviceIdType.MESH
EPSILON = 1e-06


def kernel(n, nc, rows, srcs, count, wanted, feat, tiles, noise, weight, out,
           vals, sums, dense, noise_v, weight_v, squares, xs, hp, hd, send, recv, wanted_v, wanted_s,
           cells, links_v, links, heads, head_w, acc, enc,
           local_sem, wanted_send, wanted_recv, sq_send, sq_recv, row_send, row_recv, col_send, col_recv, table_sem):
    me = lax.axis_index("row")
    col = lax.axis_index("col")
    width, nodes = feat.shape
    slots = vals.shape[0]
    f32, bf16 = jnp.float32, jnp.bfloat16

    vals_copy = pltpu.make_async_copy(tiles, vals, local_sem.at[0])
    noise_copy = pltpu.make_async_copy(noise, noise_v, local_sem.at[1])
    weight_copy = pltpu.make_async_copy(weight, weight_v, local_sem.at[2])

    barrier = pltpu.get_barrier_semaphore()

    def row_loop(body):
        def step(k, c):
            body(k)
            return c
        lax.fori_loop(1, n, step, 0)

    row_loop(lambda k: pl.semaphore_signal(
        barrier, inc=1, device_id={"row": lax.rem(me + k, n)}, device_id_type=MESH))
    for k in range(1, nc):
        pl.semaphore_signal(barrier, inc=1, device_id={"col": lax.rem(col + k, nc)}, device_id_type=MESH)
    vals_copy.start()
    noise_copy.start()
    weight_copy.start()

    left = lax.broadcasted_iota(jnp.int32, (BLK, 2 * width), 1) < width

    def block(b):
        return slice(b * BLK, (b + 1) * BLK)

    def stat(stage, x):
        squares[stage, 0] = jnp.sum(x * x, axis=0, keepdims=True)

    def square_copy(stage, k):
        return pltpu.make_async_remote_copy(
            src_ref=squares.at[stage, 0], dst_ref=squares.at[stage, k],
            send_sem=sq_send.at[stage, k], recv_sem=sq_recv.at[stage, k],
            device_id={"col": lax.rem(col + k, nc)}, device_id_type=MESH)

    def head_copy(stage, k, source):
        return pltpu.make_async_remote_copy(
            src_ref=heads.at[stage, source], dst_ref=heads.at[stage, source],
            send_sem=col_send.at[stage, k], recv_sem=col_recv.at[stage, k],
            device_id={"col": lax.rem(col + k, nc)}, device_id_type=MESH)

    def start_heads(stage):
        for k in range(1, nc):
            head_copy(stage, k, col).start()

    def wait_heads(stage):
        for k in range(1, nc):
            head_copy(stage, k, lax.rem(col + nc - k, nc)).wait_recv()

    def wanted_copy(k):
        return pltpu.make_async_remote_copy(
            src_ref=wanted.at[0], dst_ref=wanted_v.at[k],
            send_sem=wanted_send.at[k], recv_sem=wanted_recv.at[k],
            device_id={"row": lax.rem(me + k, n)}, device_id_type=MESH)

    def row_copy(hop, k):
        return pltpu.make_async_remote_copy(
            src_ref=send.at[k], dst_ref=recv.at[hop, k],
            send_sem=row_send.at[hop, k], recv_sem=row_recv.at[hop, k],
            device_id={"row": lax.rem(me + k, n)}, device_id_type=MESH)

    def inverse_norm(stage):
        for k in range(1, nc):
            square_copy(stage, k).wait_recv()
        total = squares[stage, 0]
        for k in range(1, nc):
            total = total + squares[stage, k]
        return 1.0 / jnp.sqrt(total + EPSILON)

    def normalized(stage):
        inverse = inverse_norm(stage)
        for j in range(PAIRS):
            a, b = block(2 * j), block(2 * j + 1)
            ha = (xs[:, a] * inverse[:, a]).astype(bf16)
            hb = (xs[:, b] * inverse[:, b]).astype(bf16)
            heads[stage, col, :, a] = ha
            heads[stage, col, :, b] = hb
            h = jnp.concatenate([ha.astype(f32), hb.astype(f32)], axis=0).T
            hp[j] = h.astype(bf16)
            turned = pltpu.roll(h, width, 1)
            hd[2 * j] = jnp.where(left, h, turned).astype(bf16)
            hd[2 * j + 1] = jnp.where(left, turned, h).astype(bf16)

    def send_rows(hop):
        def body(k):
            first = wanted_s[n - k, 0, me]
            second = wanted_s[n - k, 1, me]
            a = hd[first].astype(f32)
            b = hd[second].astype(f32)
            if hop > 0:
                row_copy(hop - 1, k).wait_send()
            send[k] = jnp.where(left, a, b).astype(bf16)
            row_copy(hop, k).start()
        row_loop(body)

    def spread(packed):
        p = packed.astype(f32)
        return jnp.concatenate([jnp.where(left, p, 0.0), jnp.where(left, 0.0, p)], axis=0).astype(bf16)

    def head_product(stage):
        return jnp.dot(head_w[stage], heads[stage].reshape(nc * width, nodes), preferred_element_type=f32)

    parts = cells.shape[0]
    cell = srcs[...] * BPD + rows[...]
    for p in range(parts):
        lanes = min(BLK, slots - p * BLK)
        if lanes < BLK:
            cells[p] = jnp.full((1, BLK), -1, jnp.int32)
        cells[p, :, :lanes] = cell[:, p * BLK : p * BLK + lanes]
    down = lax.broadcasted_iota(jnp.int32, (BLK, BLK), 0)
    across = lax.broadcasted_iota(jnp.int32, (BLK, BLK), 1)
    columns = [jnp.broadcast_to(cells[p], (BLK, BLK)).T for p in range(parts)]

    def latest(found):
        best = found[0]
        for f in found[1:]:
            best = jnp.maximum(best, f)
        best = jnp.max(best, axis=0, keepdims=True)
        return jnp.where(best < 0, slots, best)

    for q in range(parts):
        links_v[q] = latest([
            jnp.where((columns[p] == cells[q]) & (down + p * BLK < across + q * BLK), down + p * BLK, -1)
            for p in range(q + 1)])
    live = count[0]
    for q in range(links.shape[0] - parts):
        links_v[parts + q] = latest([
            jnp.where((columns[p] == across + q * BLK) & (down + p * BLK < live), down + p * BLK, -1)
            for p in range(parts)])
    links_copy = pltpu.make_async_copy(links_v, links, table_sem.at[1])
    links_copy.start()

    x = feat[...].astype(f32)
    xs[...] = x
    stat(0, x)

    pl.semaphore_wait(barrier, n - 1 + nc - 1)
    row_loop(lambda k: wanted_copy(k).start())
    for k in range(1, nc):
        square_copy(0, k).start()
    sums[slots] = jnp.zeros((BLK, BLK), f32)
    links_copy.wait()
    vals_copy.wait()

    def link(t, c):
        sums[t] = vals[t].astype(f32) + sums[links[t // BLK, 0, t % BLK]]
        return c

    early = slots * 3 // 8
    lax.fori_loop(0, early, link, 0, unroll=4)
    row_loop(lambda k: wanted_copy(k).wait_recv())
    table = pltpu.make_async_copy(wanted_v.at[pl.ds(1, n - 1)], wanted_s.at[pl.ds(1, n - 1)], table_sem.at[0])
    table.start()
    normalized(0)
    table.wait()
    send_rows(0)
    start_heads(0)

    lax.fori_loop(early, slots, link, 0, unroll=4)

    def lay(q, c):
        for r in range(BPD):
            for h in range(2):
                at = (2 * q + h) * BPD + r
                dense[q, r * BLK : (r + 1) * BLK, h * BLK : (h + 1) * BLK] = (
                    sums[links[parts + at // BLK, 0, at % BLK]].astype(bf16))
        return c

    lax.fori_loop(0, dense.shape[0], lay, 0)

    weight_copy.wait()
    depth = weight_v.shape[1]
    pick = (lax.broadcasted_iota(jnp.int32, (width, depth), 1)
            == lax.broadcasted_iota(jnp.int32, (width, depth), 0) + col * width).astype(f32).astype(bf16)
    for stage in range(HOPS + 1):
        head_w[stage] = lax.dot_general(
            pick, weight_v[stage], (((1,), (1,)), ((), ())), preferred_element_type=f32).astype(bf16)
    noise_copy.wait()

    for hop in range(HOPS):
        acc[...] = jnp.dot(dense[0], spread(hp[0]), preferred_element_type=f32)
        for j in range(1, PAIRS):
            acc[...] += jnp.dot(dense[j], spread(hp[j]), preferred_element_type=f32)
        if hop == 1:
            wait_heads(0)
            enc[...] = head_product(0)
        elif hop > 1:
            wait_heads(hop - 1)
            enc[...] += head_product(hop - 1)

        def arrive(k):
            row_copy(hop, k).wait_recv()
            owner = lax.rem(me + n - k, n)
            acc[...] += jnp.dot(dense[PAIRS + owner], spread(recv[hop, k]), preferred_element_type=f32)

        row_loop(arrive)
        for r in range(BPD):
            g = acc[block(r), :].T
            xs[:, block(r)] = g[:width] + g[width:] + noise_v[hop, :, block(r)]
        x = xs[...]
        stat(hop + 1, x)
        for k in range(1, nc):
            square_copy(hop + 1, k).start()
        if hop + 1 < HOPS:
            normalized(hop + 1)
            send_rows(hop + 1)
        else:
            heads[HOPS, col] = x.astype(bf16)
        start_heads(hop + 1)

    wait_heads(HOPS - 1)
    enc[...] += head_product(HOPS - 1)
    inverse = inverse_norm(HOPS)
    wait_heads(HOPS)
    out[...] = (enc[...] + head_product(HOPS) * inverse).astype(bf16)

    row_loop(lambda k: wanted_copy(k).wait_send())
    row_loop(lambda k: row_copy(HOPS - 1, k).wait_send())
    for stage in range(HOPS + 1):
        for k in range(1, nc):
            square_copy(stage, k).wait_send()
            head_copy(stage, k, col).wait_send()


def shards(n, nc, features, tile_vals, tile_rows, tile_srcs, tile_count, needed, hop_noise, enc_weight):
    local_rows, width = features.shape
    slots = tile_vals.shape[0]
    parts = pl.cdiv(slots, BLK)
    groups = pl.cdiv((BPD + n * CAP) * BPD, BLK)
    f32, bf16 = jnp.float32, jnp.bfloat16
    vmem = pl.BlockSpec(memory_space=pltpu.VMEM)
    smem = pl.BlockSpec(memory_space=pltpu.SMEM)
    anyspace = pl.BlockSpec(memory_space=pl.ANY)
    sem = pltpu.SemaphoreType.DMA
    pair = (BLK, 2 * width)
    result = pl.pallas_call(
        functools.partial(kernel, n, nc),
        out_shape=jax.ShapeDtypeStruct((width, local_rows), bf16),
        in_specs=[vmem, vmem, smem, anyspace, vmem, anyspace, anyspace, anyspace],
        out_specs=vmem,
        scratch_shapes=[
            pltpu.VMEM(tile_vals.shape, bf16),
            pltpu.VMEM((slots + 1, BLK, BLK), f32),
            pltpu.VMEM((PAIRS + n, local_rows, 2 * BLK), bf16),
            pltpu.VMEM((HOPS, width, local_rows), f32),
            pltpu.VMEM(enc_weight.shape, bf16),
            pltpu.VMEM((HOPS + 1, nc, 1, local_rows), f32),
            pltpu.VMEM((width, local_rows), f32),
            pltpu.VMEM((PAIRS,) + pair, bf16),
            pltpu.VMEM((BPD,) + pair, bf16),
            pltpu.VMEM((n,) + pair, bf16),
            pltpu.VMEM((HOPS, n) + pair, bf16),
            pltpu.VMEM((n, CAP, n), jnp.int32),
            pltpu.SMEM((n, CAP, n), jnp.int32),
            pltpu.VMEM((parts, 1, BLK), jnp.int32),
            pltpu.VMEM((parts + groups, 1, BLK), jnp.int32),
            pltpu.SMEM((parts + groups, 1, BLK), jnp.int32),
            pltpu.VMEM((HOPS + 1, nc, width, local_rows), bf16),
            pltpu.VMEM((HOPS + 1, width, nc * width), bf16),
            pltpu.VMEM((local_rows, 2 * width), f32),
            pltpu.VMEM((width, local_rows), f32),
            sem((3,)),
            sem((n,)), sem((n,)),
            sem((HOPS + 1, nc)), sem((HOPS + 1, nc)),
            sem((HOPS, n)), sem((HOPS, n)),
            sem((HOPS + 1, nc)), sem((HOPS + 1, nc)),
            sem((2,)),
        ],
        compiler_params=pltpu.CompilerParams(
            collective_id=0, has_side_effects=True, vmem_limit_bytes=62 * 2**20),
    )(tile_rows, tile_srcs, tile_count, needed.transpose(0, 2, 1), features.T, tile_vals,
      hop_noise.transpose(0, 2, 1), enc_weight)
    return result.T


def solution(mesh):
    n, nc = mesh.shape["row"], mesh.shape["col"]
    in_specs = (
        P("row", "col"),
        P("row", None, None),
        P("row", None),
        P("row", None),
        P("row"),
        P("row", None, None),
        P(None, "row", "col"),
        P(),
    )
    return jax.shard_map(functools.partial(shards, n, nc), mesh=mesh, in_specs=in_specs,
                         out_specs=P("row", "col"), check_vma=False)
```

```python
import functools

import jax
import jax.numpy as jnp
from jax import lax
from jax.experimental import pallas as pl
from jax.experimental.pallas import tpu as pltpu
from jax.sharding import PartitionSpec as P

BLK = 128
BPD = 8
CAP = 2
HOPS = 2
PAIRS = BPD // 2
MESH = pl.DeviceIdType.MESH
EPSILON = 1e-06


def kernel(n, nc, rows, srcs, count, wanted, feat, tiles, noise, weight, out,
           vals, sums, dense, noise_v, weight_v, squares, xs, hp, raw, scale, send, recv, scale_send, scale_recv, wanted_v, wanted_s,
           cells, links_v, links, heads, last, head_w, acc, enc,
           local_sem, wanted_send, wanted_recv, sq_send, sq_recv, row_send, row_recv, tail_send, tail_recv,
           col_send, col_recv, last_send, last_recv, table_sem):
    me = lax.axis_index("row")
    col = lax.axis_index("col")
    width, nodes = feat.shape
    half = nodes // 2
    slots = vals.shape[0]
    f32, bf16 = jnp.float32, jnp.bfloat16

    vals_copy = pltpu.make_async_copy(tiles, vals, local_sem.at[0])
    noise_copy = pltpu.make_async_copy(noise, noise_v, local_sem.at[1])
    weight_copy = pltpu.make_async_copy(weight, weight_v, local_sem.at[2])

    barrier = pltpu.get_barrier_semaphore()

    def row_loop(body):
        def step(k, c):
            body(k)
            return c
        lax.fori_loop(1, n, step, 0)

    row_loop(lambda k: pl.semaphore_signal(
        barrier, inc=1, device_id={"row": lax.rem(me + k, n)}, device_id_type=MESH))
    for k in range(1, nc):
        pl.semaphore_signal(barrier, inc=1, device_id={"col": lax.rem(col + k, nc)}, device_id_type=MESH)
    vals_copy.start()
    noise_copy.start()
    weight_copy.start()

    left = lax.broadcasted_iota(jnp.int32, (BLK, 2 * width), 1) < width

    def block(b):
        return slice(b * BLK, (b + 1) * BLK)

    def stat(stage, x):
        squares[stage, 0] = jnp.sum(x * x, axis=0, keepdims=True)

    def square_copy(stage, k):
        return pltpu.make_async_remote_copy(
            src_ref=squares.at[stage, 0], dst_ref=squares.at[stage, k],
            send_sem=sq_send.at[stage, k], recv_sem=sq_recv.at[stage, k],
            device_id={"col": lax.rem(col + k, nc)}, device_id_type=MESH)

    def head_copy(stage, k, source):
        return pltpu.make_async_remote_copy(
            src_ref=heads.at[stage, source], dst_ref=heads.at[stage, source],
            send_sem=col_send.at[stage, k], recv_sem=col_recv.at[stage, k],
            device_id={"col": lax.rem(col + k, nc)}, device_id_type=MESH)

    def start_heads(stage):
        for k in range(1, nc):
            head_copy(stage, k, col).start()

    def wait_heads(stage):
        for k in range(1, nc):
            head_copy(stage, k, lax.rem(col + nc - k, nc)).wait_recv()

    def wanted_copy(k):
        return pltpu.make_async_remote_copy(
            src_ref=wanted.at[0], dst_ref=wanted_v.at[k],
            send_sem=wanted_send.at[k], recv_sem=wanted_recv.at[k],
            device_id={"row": lax.rem(me + k, n)}, device_id_type=MESH)

    def row_copy(hop, k):
        return pltpu.make_async_remote_copy(
            src_ref=send.at[k], dst_ref=recv.at[hop, k],
            send_sem=row_send.at[hop, k], recv_sem=row_recv.at[hop, k],
            device_id={"row": lax.rem(me + k, n)}, device_id_type=MESH)

    def scale_copy(hop, k):
        return pltpu.make_async_remote_copy(
            src_ref=scale_send.at[hop, k], dst_ref=scale_recv.at[hop, k],
            send_sem=tail_send.at[hop, k], recv_sem=tail_recv.at[hop, k],
            device_id={"row": lax.rem(me + k, n)}, device_id_type=MESH)

    def last_copy(part, way, source, peer):
        return pltpu.make_async_remote_copy(
            src_ref=last.at[part, source], dst_ref=last.at[part, source],
            send_sem=last_send.at[part, way], recv_sem=last_recv.at[part, way],
            device_id={"col": peer}, device_id_type=MESH)

    def far_first(i):
        return n // 2 + (1 - 2 * lax.rem(i, 2)) * ((i + 1) // 2)

    def inverse_norm(stage):
        for k in range(1, nc):
            square_copy(stage, k).wait_recv()
        total = squares[stage, 0]
        for k in range(1, nc):
            total = total + squares[stage, k]
        return 1.0 / jnp.sqrt(total + EPSILON)

    def normalized(stage):
        inverse = inverse_norm(stage)
        for r in range(BPD):
            scale[r] = inverse[:, block(r)]
        for j in range(PAIRS):
            a, b = block(2 * j), block(2 * j + 1)
            ha = (xs[:, a] * inverse[:, a]).astype(bf16)
            hb = (xs[:, b] * inverse[:, b]).astype(bf16)
            heads[stage, col, :, a] = ha
            heads[stage, col, :, b] = hb
            hp[j] = jnp.concatenate([ha.astype(f32), hb.astype(f32)], axis=0).T.astype(bf16)

    def send_rows(hop):
        def body(i, c):
            k = far_first(i)
            if hop > 0:
                row_copy(hop - 1, k).wait_send()
            send[k, :width] = raw[wanted_s[n - k, 0, me]]
            send[k, width:] = raw[wanted_s[n - k, 1, me]]
            row_copy(hop, k).start()
            return c
        lax.fori_loop(0, n - 1, body, 0)

    def send_scales(hop):
        def body(i, c):
            k = far_first(i)
            scale_send[hop, k, 0] = scale[wanted_s[n - k, 0, me]]
            scale_send[hop, k, 1] = scale[wanted_s[n - k, 1, me]]
            scale_copy(hop, k).start()
            return c
        lax.fori_loop(0, n - 1, body, 0)

    def spread(packed):
        p = packed.astype(f32)
        return jnp.concatenate([jnp.where(left, p, 0.0), jnp.where(left, 0.0, p)], axis=0).astype(bf16)

    def head_product(stage):
        return jnp.dot(head_w[stage], heads[stage].reshape(nc * width, nodes), preferred_element_type=f32)

    parts = cells.shape[0]
    cell = srcs[...] * BPD + rows[...]
    for p in range(parts):
        lanes = min(BLK, slots - p * BLK)
        if lanes < BLK:
            cells[p] = jnp.full((1, BLK), -1, jnp.int32)
        cells[p, :, :lanes] = cell[:, p * BLK : p * BLK + lanes]
    down = lax.broadcasted_iota(jnp.int32, (BLK, BLK), 0)
    across = lax.broadcasted_iota(jnp.int32, (BLK, BLK), 1)
    columns = [jnp.broadcast_to(cells[p], (BLK, BLK)).T for p in range(parts)]

    def latest(found):
        best = found[0]
        for f in found[1:]:
            best = jnp.maximum(best, f)
        best = jnp.max(best, axis=0, keepdims=True)
        return jnp.where(best < 0, slots, best)

    for q in range(parts):
        links_v[q] = latest([
            jnp.where((columns[p] == cells[q]) & (down + p * BLK < across + q * BLK), down + p * BLK, -1)
            for p in range(q + 1)])
    live = count[0]
    for q in range(links.shape[0] - parts):
        links_v[parts + q] = latest([
            jnp.where((columns[p] == across + q * BLK) & (down + p * BLK < live), down + p * BLK, -1)
            for p in range(parts)])
    links_copy = pltpu.make_async_copy(links_v, links, table_sem.at[1])
    links_copy.start()

    x = feat[...].astype(f32)
    xs[...] = x
    for r in range(BPD):
        raw[r] = feat[:, block(r)]
    stat(0, x)

    pl.semaphore_wait(barrier, n - 1 + nc - 1)
    row_loop(lambda k: wanted_copy(k).start())
    for k in range(1, nc):
        square_copy(0, k).start()
    sums[slots] = jnp.zeros((BLK, BLK), f32)
    links_copy.wait()
    vals_copy.wait()

    def link(t, c):
        sums[t] = vals[t].astype(f32) + sums[links[t // BLK, 0, t % BLK]]
        return c

    early = slots * 3 // 8
    lax.fori_loop(0, early, link, 0, unroll=4)
    row_loop(lambda k: wanted_copy(k).wait_recv())
    table = pltpu.make_async_copy(wanted_v.at[pl.ds(1, n - 1)], wanted_s.at[pl.ds(1, n - 1)], table_sem.at[0])
    table.start()
    table.wait()
    send_rows(0)
    normalized(0)
    send_scales(0)
    start_heads(0)

    lax.fori_loop(early, slots, link, 0, unroll=4)

    def lay(q, c):
        for r in range(BPD):
            for h in range(2):
                at = (2 * q + h) * BPD + r
                dense[q, r * BLK : (r + 1) * BLK, h * BLK : (h + 1) * BLK] = (
                    sums[links[parts + at // BLK, 0, at % BLK]].astype(bf16))
        return c

    lax.fori_loop(0, dense.shape[0], lay, 0)

    weight_copy.wait()
    depth = weight_v.shape[1]
    pick = (lax.broadcasted_iota(jnp.int32, (width, depth), 1)
            == lax.broadcasted_iota(jnp.int32, (width, depth), 0) + col * width).astype(f32).astype(bf16)
    for stage in range(HOPS + 1):
        head_w[stage] = lax.dot_general(
            pick, weight_v[stage], (((1,), (1,)), ((), ())), preferred_element_type=f32).astype(bf16)
    noise_copy.wait()

    for hop in range(HOPS):
        acc[...] = jnp.dot(dense[0], spread(hp[0]), preferred_element_type=f32)
        for j in range(1, PAIRS):
            acc[...] += jnp.dot(dense[j], spread(hp[j]), preferred_element_type=f32)
        if hop == 1:
            wait_heads(0)
            enc[...] = head_product(0)
        elif hop > 1:
            wait_heads(hop - 1)
            enc[...] += head_product(hop - 1)

        def arrive(i, c):
            k = far_first(n - 2 - i)
            row_copy(hop, k).wait_recv()
            scale_copy(hop, k).wait_recv()
            both = jnp.concatenate(
                [jnp.broadcast_to(scale_recv[hop, k, 0], (width, BLK)),
                 jnp.broadcast_to(scale_recv[hop, k, 1], (width, BLK))], axis=0)
            h = (recv[hop, k].astype(f32) * both).astype(bf16)
            owner = lax.rem(me + n - k, n)
            acc[...] += jnp.dot(dense[PAIRS + owner], spread(h.astype(f32).T), preferred_element_type=f32)
            return c

        lax.fori_loop(0, n - 1, arrive, 0)
        for r in range(BPD):
            g = acc[block(r), :].T
            x = g[:width] + g[width:] + noise_v[hop, :, block(r)]
            xs[:, block(r)] = x
            if hop + 1 < HOPS:
                raw[r] = x.astype(bf16)
            else:
                last[r * BLK // half, col, :, r * BLK % half : r * BLK % half + BLK] = x.astype(bf16)
        if hop + 1 < HOPS:
            send_rows(hop + 1)
        stat(hop + 1, xs[...])
        for k in range(1, nc):
            square_copy(hop + 1, k).start()
        if hop + 1 < HOPS:
            normalized(hop + 1)
            send_scales(hop + 1)
            start_heads(hop + 1)

    near = col + 1 - 2 * lax.rem(col, 2)
    far = lax.rem(col + 2, nc)
    both = lax.rem(near + 2, nc)
    for part in range(2):
        last_copy(part, 0, col, far).start()
    for part in range(2):
        last_copy(part, 1, col, near).start()
    wait_heads(HOPS - 1)
    enc[...] += head_product(HOPS - 1)
    inverse = inverse_norm(HOPS)
    for part in range(2):
        last_copy(part, 0, far, far).wait_recv()
        last_copy(part, 2, far, near).start()
    for part in range(2):
        lanes = slice(part * half, (part + 1) * half)
        last_copy(part, 1, near, near).wait_recv()
        last_copy(part, 2, both, near).wait_recv()
        product = jnp.dot(head_w[HOPS], last[part].reshape(nc * width, half), preferred_element_type=f32)
        out[:, lanes] = enc[:, lanes] + product * inverse[:, lanes]

    row_loop(lambda k: wanted_copy(k).wait_send())
    row_loop(lambda k: row_copy(HOPS - 1, k).wait_send())
    for stage in range(HOPS + 1):
        for k in range(1, nc):
            square_copy(stage, k).wait_send()
    for stage in range(HOPS):
        row_loop(lambda k: scale_copy(stage, k).wait_send())
        for k in range(1, nc):
            head_copy(stage, k, col).wait_send()
    for part in range(2):
        last_copy(part, 0, col, far).wait_send()
        last_copy(part, 1, col, near).wait_send()
        last_copy(part, 2, far, near).wait_send()


def shards(n, nc, features, tile_vals, tile_rows, tile_srcs, tile_count, needed, hop_noise, enc_weight):
    local_rows, width = features.shape
    slots = tile_vals.shape[0]
    parts = pl.cdiv(slots, BLK)
    groups = pl.cdiv((BPD + n * CAP) * BPD, BLK)
    f32, bf16 = jnp.float32, jnp.bfloat16
    vmem = pl.BlockSpec(memory_space=pltpu.VMEM)
    smem = pl.BlockSpec(memory_space=pltpu.SMEM)
    anyspace = pl.BlockSpec(memory_space=pl.ANY)
    sem = pltpu.SemaphoreType.DMA
    pair = (BLK, 2 * width)
    result = pl.pallas_call(
        functools.partial(kernel, n, nc),
        out_shape=jax.ShapeDtypeStruct((width, local_rows), f32),
        in_specs=[vmem, vmem, smem, anyspace, vmem, anyspace, anyspace, anyspace],
        out_specs=vmem,
        scratch_shapes=[
            pltpu.VMEM(tile_vals.shape, bf16),
            pltpu.VMEM((slots + 1, BLK, BLK), f32),
            pltpu.VMEM((PAIRS + n, local_rows, 2 * BLK), bf16),
            pltpu.VMEM((HOPS, width, local_rows), f32),
            pltpu.VMEM(enc_weight.shape, bf16),
            pltpu.VMEM((HOPS + 1, nc, 1, local_rows), f32),
            pltpu.VMEM((width, local_rows), f32),
            pltpu.VMEM((PAIRS,) + pair, bf16),
            pltpu.VMEM((BPD, width, BLK), bf16),
            pltpu.VMEM((BPD, 1, BLK), f32),
            pltpu.VMEM((n, 2 * width, BLK), bf16),
            pltpu.VMEM((HOPS, n, 2 * width, BLK), bf16),
            pltpu.VMEM((HOPS, n, CAP, 1, BLK), f32),
            pltpu.VMEM((HOPS, n, CAP, 1, BLK), f32),
            pltpu.VMEM((n, CAP, n), jnp.int32),
            pltpu.SMEM((n, CAP, n), jnp.int32),
            pltpu.VMEM((parts, 1, BLK), jnp.int32),
            pltpu.VMEM((parts + groups, 1, BLK), jnp.int32),
            pltpu.SMEM((parts + groups, 1, BLK), jnp.int32),
            pltpu.VMEM((HOPS, nc, width, local_rows), bf16),
            pltpu.VMEM((2, nc, width, local_rows // 2), bf16),
            pltpu.VMEM((HOPS + 1, width, nc * width), bf16),
            pltpu.VMEM((local_rows, 2 * width), f32),
            pltpu.VMEM((width, local_rows), f32),
            sem((3,)),
            sem((n,)), sem((n,)),
            sem((HOPS + 1, nc)), sem((HOPS + 1, nc)),
            sem((HOPS, n)), sem((HOPS, n)),
            sem((HOPS, n)), sem((HOPS, n)),
            sem((HOPS, nc)), sem((HOPS, nc)),
            sem((2, 3)), sem((2, 3)),
            sem((2,)),
        ],
        compiler_params=pltpu.CompilerParams(
            collective_id=0, has_side_effects=True, vmem_limit_bytes=62 * 2**20),
    )(tile_rows, tile_srcs, tile_count, needed.transpose(0, 2, 1), features.T, tile_vals,
      hop_noise.transpose(0, 2, 1), enc_weight)
    return result.T.astype(bf16)


def solution(mesh):
    n, nc = mesh.shape["row"], mesh.shape["col"]
    in_specs = (
        P("row", "col"),
        P("row", None, None),
        P("row", None),
        P("row", None),
        P("row"),
        P("row", None, None),
        P(None, "row", "col"),
        P(),
    )
    return jax.shard_map(functools.partial(shards, n, nc), mesh=mesh, in_specs=in_specs,
                         out_specs=P("row", "col"), check_vma=False)
```

```python
import functools

import jax
import jax.numpy as jnp
from jax import lax
from jax.experimental import pallas as pl
from jax.experimental.pallas import tpu as pltpu
from jax.sharding import PartitionSpec as P

BLK = 128
BPD = 8
CAP = 2
HOPS = 2
PAIRS = BPD // 2
MESH = pl.DeviceIdType.MESH
EPSILON = 1e-06


def kernel(n, nc, rows, srcs, count, wanted, feat, tiles, noise, weight, out,
           vals, sums, dense, noise_v, weight_v, squares, xs, raw, scale, send, recv, scale_send, scale_recv, wanted_v, wanted_s,
           cells, links_v, links, heads, last, head_w, acc, enc,
           local_sem, wanted_send, wanted_recv, sq_send, sq_recv, row_send, row_recv, tail_send, tail_recv,
           col_send, col_recv, last_send, last_recv, table_sem):
    me = lax.axis_index("row")
    col = lax.axis_index("col")
    width, nodes = feat.shape
    half = nodes // 2
    slots = vals.shape[0]
    f32, bf16 = jnp.float32, jnp.bfloat16

    vals_copy = pltpu.make_async_copy(tiles, vals, local_sem.at[0])
    noise_copy = pltpu.make_async_copy(noise, noise_v, local_sem.at[1])
    weight_copy = pltpu.make_async_copy(weight, weight_v, local_sem.at[2])

    barrier = pltpu.get_barrier_semaphore()

    def row_loop(body):
        def step(k, c):
            body(k)
            return c
        lax.fori_loop(1, n, step, 0)

    row_loop(lambda k: pl.semaphore_signal(
        barrier, inc=1, device_id={"row": lax.rem(me + k, n)}, device_id_type=MESH))
    for k in range(1, nc):
        pl.semaphore_signal(barrier, inc=1, device_id={"col": lax.rem(col + k, nc)}, device_id_type=MESH)
    vals_copy.start()
    noise_copy.start()
    weight_copy.start()

    def block(b):
        return slice(b * BLK, (b + 1) * BLK)

    def stat(stage, x):
        squares[stage, 0] = jnp.sum(x * x, axis=0, keepdims=True)

    def square_copy(stage, k):
        return pltpu.make_async_remote_copy(
            src_ref=squares.at[stage, 0], dst_ref=squares.at[stage, k],
            send_sem=sq_send.at[stage, k], recv_sem=sq_recv.at[stage, k],
            device_id={"col": lax.rem(col + k, nc)}, device_id_type=MESH)

    def head_copy(stage, k, source):
        return pltpu.make_async_remote_copy(
            src_ref=heads.at[stage, source], dst_ref=heads.at[stage, source],
            send_sem=col_send.at[stage, k], recv_sem=col_recv.at[stage, k],
            device_id={"col": lax.rem(col + k, nc)}, device_id_type=MESH)

    def start_heads(stage):
        for k in range(1, nc):
            head_copy(stage, k, col).start()

    def wait_heads(stage):
        for k in range(1, nc):
            head_copy(stage, k, lax.rem(col + nc - k, nc)).wait_recv()

    def wanted_copy(k):
        return pltpu.make_async_remote_copy(
            src_ref=wanted.at[0], dst_ref=wanted_v.at[k],
            send_sem=wanted_send.at[k], recv_sem=wanted_recv.at[k],
            device_id={"row": lax.rem(me + k, n)}, device_id_type=MESH)

    def row_copy(hop, k):
        return pltpu.make_async_remote_copy(
            src_ref=send.at[k], dst_ref=recv.at[hop, k],
            send_sem=row_send.at[hop, k], recv_sem=row_recv.at[hop, k],
            device_id={"row": lax.rem(me + k, n)}, device_id_type=MESH)

    def scale_copy(hop, k):
        return pltpu.make_async_remote_copy(
            src_ref=scale_send.at[hop, k], dst_ref=scale_recv.at[hop, k],
            send_sem=tail_send.at[hop, k], recv_sem=tail_recv.at[hop, k],
            device_id={"row": lax.rem(me + k, n)}, device_id_type=MESH)

    def last_copy(part, way, source, peer):
        return pltpu.make_async_remote_copy(
            src_ref=last.at[part, source], dst_ref=last.at[part, source],
            send_sem=last_send.at[part, way], recv_sem=last_recv.at[part, way],
            device_id={"col": peer}, device_id_type=MESH)

    def far_first(i):
        return n // 2 + (1 - 2 * lax.rem(i, 2)) * ((i + 1) // 2)

    def inverse_norm(stage):
        for k in range(1, nc):
            square_copy(stage, k).wait_recv()
        total = squares[stage, 0]
        for k in range(1, nc):
            total = total + squares[stage, k]
        return 1.0 / jnp.sqrt(total + EPSILON)

    def normalized(stage):
        inverse = inverse_norm(stage)
        for r in range(BPD):
            scale[r] = inverse[:, block(r)]
        heads[stage, col] = (xs[...] * inverse).astype(bf16)

    def send_rows(hop):
        def body(i, c):
            k = far_first(i)
            if hop > 0:
                row_copy(hop - 1, k).wait_send()
            send[k, :width] = raw[wanted_s[n - k, 0, me]]
            send[k, width:] = raw[wanted_s[n - k, 1, me]]
            row_copy(hop, k).start()
            return c
        lax.fori_loop(0, n - 1, body, 0)

    def send_scales(hop):
        def body(i, c):
            k = far_first(i)
            scale_send[hop, k, 0] = scale[wanted_s[n - k, 0, me]]
            scale_send[hop, k, 1] = scale[wanted_s[n - k, 1, me]]
            scale_copy(hop, k).start()
            return c
        lax.fori_loop(0, n - 1, body, 0)

    def tile_product(rows_t, q):
        return lax.dot_general(rows_t, dense[q], (((1,), (1,)), ((), ())), preferred_element_type=f32)

    def head_product(stage):
        return jnp.dot(head_w[stage], heads[stage].reshape(nc * width, nodes), preferred_element_type=f32)

    parts = cells.shape[0]
    cell = srcs[...] * BPD + rows[...]
    for p in range(parts):
        lanes = min(BLK, slots - p * BLK)
        if lanes < BLK:
            cells[p] = jnp.full((1, BLK), -1, jnp.int32)
        cells[p, :, :lanes] = cell[:, p * BLK : p * BLK + lanes]
    down = lax.broadcasted_iota(jnp.int32, (BLK, BLK), 0)
    across = lax.broadcasted_iota(jnp.int32, (BLK, BLK), 1)
    columns = [jnp.broadcast_to(cells[p], (BLK, BLK)).T for p in range(parts)]

    def latest(found):
        best = found[0]
        for f in found[1:]:
            best = jnp.maximum(best, f)
        best = jnp.max(best, axis=0, keepdims=True)
        return jnp.where(best < 0, slots, best)

    for q in range(parts):
        links_v[q] = latest([
            jnp.where((columns[p] == cells[q]) & (down + p * BLK < across + q * BLK), down + p * BLK, -1)
            for p in range(q + 1)])
    live = count[0]
    for q in range(links.shape[0] - parts):
        links_v[parts + q] = latest([
            jnp.where((columns[p] == across + q * BLK) & (down + p * BLK < live), down + p * BLK, -1)
            for p in range(parts)])
    links_copy = pltpu.make_async_copy(links_v, links, table_sem.at[1])
    links_copy.start()

    x = feat[...].astype(f32)
    xs[...] = x
    for r in range(BPD):
        raw[r] = feat[:, block(r)]
    stat(0, x)

    pl.semaphore_wait(barrier, n - 1 + nc - 1)
    row_loop(lambda k: wanted_copy(k).start())
    for k in range(1, nc):
        square_copy(0, k).start()
    sums[slots] = jnp.zeros((BLK, BLK), f32)
    links_copy.wait()
    vals_copy.wait()

    def link(t, c):
        sums[t] = vals[t].astype(f32) + sums[links[t // BLK, 0, t % BLK]]
        return c

    early = slots * 3 // 8
    lax.fori_loop(0, early, link, 0, unroll=4)
    row_loop(lambda k: wanted_copy(k).wait_recv())
    table = pltpu.make_async_copy(wanted_v.at[pl.ds(1, n - 1)], wanted_s.at[pl.ds(1, n - 1)], table_sem.at[0])
    table.start()
    table.wait()
    send_rows(0)
    normalized(0)
    send_scales(0)
    start_heads(0)

    lax.fori_loop(early, slots, link, 0, unroll=4)

    def lay(q, c):
        for r in range(BPD):
            for h in range(2):
                at = (2 * q + h) * BPD + r
                dense[q, r * BLK : (r + 1) * BLK, h * BLK : (h + 1) * BLK] = (
                    sums[links[parts + at // BLK, 0, at % BLK]].astype(bf16))
        return c

    lax.fori_loop(0, dense.shape[0], lay, 0)

    weight_copy.wait()
    depth = weight_v.shape[1]
    pick = (lax.broadcasted_iota(jnp.int32, (width, depth), 1)
            == lax.broadcasted_iota(jnp.int32, (width, depth), 0) + col * width).astype(f32).astype(bf16)
    for stage in range(HOPS + 1):
        head_w[stage] = lax.dot_general(
            pick, weight_v[stage], (((1,), (1,)), ((), ())), preferred_element_type=f32).astype(bf16)
    noise_copy.wait()

    for hop in range(HOPS):
        acc[...] = noise_v[hop]
        for j in range(PAIRS):
            acc[...] += tile_product(heads[hop, col, :, 2 * j * BLK : (2 * j + 2) * BLK], j)
        if hop == 1:
            wait_heads(0)
            enc[...] = head_product(0)
        elif hop > 1:
            wait_heads(hop - 1)
            enc[...] += head_product(hop - 1)

        def arrive(i, c):
            k = far_first(n - 2 - i)
            row_copy(hop, k).wait_recv()
            scale_copy(hop, k).wait_recv()
            first = (recv[hop, k, :width].astype(f32) * scale_recv[hop, k, 0]).astype(bf16)
            second = (recv[hop, k, width:].astype(f32) * scale_recv[hop, k, 1]).astype(bf16)
            owner = lax.rem(me + n - k, n)
            acc[...] += tile_product(jnp.concatenate([first, second], axis=1), PAIRS + owner)
            return c

        lax.fori_loop(0, n - 1, arrive, 0)
        for r in range(BPD):
            x = acc[:, block(r)]
            xs[:, block(r)] = x
            if hop + 1 < HOPS:
                raw[r] = x.astype(bf16)
            else:
                last[r * BLK // half, col, :, r * BLK % half : r * BLK % half + BLK] = x.astype(bf16)
        if hop + 1 < HOPS:
            send_rows(hop + 1)
        stat(hop + 1, xs[...])
        for k in range(1, nc):
            square_copy(hop + 1, k).start()
        if hop + 1 < HOPS:
            normalized(hop + 1)
            send_scales(hop + 1)
            start_heads(hop + 1)

    near = col + 1 - 2 * lax.rem(col, 2)
    far = lax.rem(col + 2, nc)
    both = lax.rem(near + 2, nc)
    for part in range(2):
        last_copy(part, 0, col, far).start()
    for part in range(2):
        last_copy(part, 1, col, near).start()
    wait_heads(HOPS - 1)
    enc[...] += head_product(HOPS - 1)
    inverse = inverse_norm(HOPS)
    for part in range(2):
        last_copy(part, 0, far, far).wait_recv()
        last_copy(part, 2, far, near).start()
    for part in range(2):
        lanes = slice(part * half, (part + 1) * half)
        last_copy(part, 1, near, near).wait_recv()
        last_copy(part, 2, both, near).wait_recv()
        product = jnp.dot(head_w[HOPS], last[part].reshape(nc * width, half), preferred_element_type=f32)
        out[:, lanes] = enc[:, lanes] + product * inverse[:, lanes]

    row_loop(lambda k: wanted_copy(k).wait_send())
    row_loop(lambda k: row_copy(HOPS - 1, k).wait_send())
    for stage in range(HOPS + 1):
        for k in range(1, nc):
            square_copy(stage, k).wait_send()
    for stage in range(HOPS):
        row_loop(lambda k: scale_copy(stage, k).wait_send())
        for k in range(1, nc):
            head_copy(stage, k, col).wait_send()
    for part in range(2):
        last_copy(part, 0, col, far).wait_send()
        last_copy(part, 1, col, near).wait_send()
        last_copy(part, 2, far, near).wait_send()


def shards(n, nc, features, tile_vals, tile_rows, tile_srcs, tile_count, needed, hop_noise, enc_weight):
    local_rows, width = features.shape
    slots = tile_vals.shape[0]
    parts = pl.cdiv(slots, BLK)
    groups = pl.cdiv((BPD + n * CAP) * BPD, BLK)
    f32, bf16 = jnp.float32, jnp.bfloat16
    vmem = pl.BlockSpec(memory_space=pltpu.VMEM)
    smem = pl.BlockSpec(memory_space=pltpu.SMEM)
    anyspace = pl.BlockSpec(memory_space=pl.ANY)
    sem = pltpu.SemaphoreType.DMA
    result = pl.pallas_call(
        functools.partial(kernel, n, nc),
        out_shape=jax.ShapeDtypeStruct((width, local_rows), f32),
        in_specs=[vmem, vmem, smem, anyspace, vmem, anyspace, anyspace, anyspace],
        out_specs=vmem,
        scratch_shapes=[
            pltpu.VMEM(tile_vals.shape, bf16),
            pltpu.VMEM((slots + 1, BLK, BLK), f32),
            pltpu.VMEM((PAIRS + n, local_rows, 2 * BLK), bf16),
            pltpu.VMEM((HOPS, width, local_rows), f32),
            pltpu.VMEM(enc_weight.shape, bf16),
            pltpu.VMEM((HOPS + 1, nc, 1, local_rows), f32),
            pltpu.VMEM((width, local_rows), f32),
            pltpu.VMEM((BPD, width, BLK), bf16),
            pltpu.VMEM((BPD, 1, BLK), f32),
            pltpu.VMEM((n, 2 * width, BLK), bf16),
            pltpu.VMEM((HOPS, n, 2 * width, BLK), bf16),
            pltpu.VMEM((HOPS, n, CAP, 1, BLK), f32),
            pltpu.VMEM((HOPS, n, CAP, 1, BLK), f32),
            pltpu.VMEM((n, CAP, n), jnp.int32),
            pltpu.SMEM((n, CAP, n), jnp.int32),
            pltpu.VMEM((parts, 1, BLK), jnp.int32),
            pltpu.VMEM((parts + groups, 1, BLK), jnp.int32),
            pltpu.SMEM((parts + groups, 1, BLK), jnp.int32),
            pltpu.VMEM((HOPS, nc, width, local_rows), bf16),
            pltpu.VMEM((2, nc, width, local_rows // 2), bf16),
            pltpu.VMEM((HOPS + 1, width, nc * width), bf16),
            pltpu.VMEM((width, local_rows), f32),
            pltpu.VMEM((width, local_rows), f32),
            sem((3,)),
            sem((n,)), sem((n,)),
            sem((HOPS + 1, nc)), sem((HOPS + 1, nc)),
            sem((HOPS, n)), sem((HOPS, n)),
            sem((HOPS, n)), sem((HOPS, n)),
            sem((HOPS, nc)), sem((HOPS, nc)),
            sem((2, 3)), sem((2, 3)),
            sem((2,)),
        ],
        compiler_params=pltpu.CompilerParams(
            collective_id=0, has_side_effects=True, vmem_limit_bytes=62 * 2**20),
    )(tile_rows, tile_srcs, tile_count, needed.transpose(0, 2, 1), features.T, tile_vals,
      hop_noise.transpose(0, 2, 1), enc_weight)
    return result.T.astype(bf16)


def solution(mesh):
    n, nc = mesh.shape["row"], mesh.shape["col"]
    in_specs = (
        P("row", "col"),
        P("row", None, None),
        P("row", None),
        P("row", None),
        P("row"),
        P("row", None, None),
        P(None, "row", "col"),
        P(),
    )
    return jax.shard_map(functools.partial(shards, n, nc), mesh=mesh, in_specs=in_specs,
                         out_specs=P("row", "col"), check_vma=False)
```
